256 devices in a mesh: hid: 16 (over z, x_hi), wid: 16 (over y, x_lo, core).
Axes of the slice: x: 4 (x_hi: 2, x_lo: 2; x = x_hi * 2 + x_lo), y: 4, z: 8, core: 2. Of those that a mesh axis runs over, the one named last changes fastest.
Arguments:
- tokens: bfloat16 [1024, 8192], P('hid', 'wid'), may hold values from -6 to 6
- grad_out: bfloat16 [1024, 8192], P('hid', 'wid'), may hold values from -6 to 6
- gate_codes: bfloat16 [8192, 14336], P('wid', 'hid'), may hold values from -7.5 to 7.5, as said below
- gate_scale: float32 [64, 112], P('wid', 'hid'), may hold values from 0.0022097088 to 0.008838835
- up_codes: bfloat16 [8192, 14336], P('wid', 'hid'), may hold values from -7.5 to 7.5, as said below
- up_scale: float32 [64, 112], P('wid', 'hid'), may hold values from 0.0022097088 to 0.008838835
- down_codes: bfloat16 [14336, 8192], P('hid', 'wid'), may hold values from -7.5 to 7.5, as said below
- down_scale: float32 [112, 64], P('hid', 'wid'), may hold values from 0.0016703828 to 0.006681531
Outputs:
- grad_tokens: bfloat16 [1024, 8192], P('hid', 'wid')
- grad_gate: bfloat16 [8192, 14336], P('wid', 'hid')
- grad_up: bfloat16 [8192, 14336], P('wid', 'hid')
- grad_down: bfloat16 [14336, 8192], P('hid', 'wid')
- block_norms: float32 [3, 64, 112], P(None, 'wid', 'hid')
The draws below stay inside these ranges and needn't reach their ends.
Inputs may be any that keep to these rules, and one draw needn't show every extreme that they name: Every entry of gate_codes is an e4m3 value: a sign times 2 to a power from -2 to 2 times 1 + m / 8 with m from 0 to 7. Every entry of up_codes is an e4m3 value of the same kind. Every entry of down_codes is an e4m3 value of the same kind.
All inputs are finite; a program needn't handle non-finite values.
Results may differ from the reference program's by a relative error of at most 0.039.
Values may be sent and summed in bfloat16 or wider, within the bound.
A program may use at most 64 MiB of HBM per device.

```python
import math
import jax
import jax.numpy as jnp
from jax import lax

D = 8192
FF = 14336
BLK = 128
TOKENS = 1024
N_HID = 16
N_WID = 16


def code_grid(key, rows, cols):
    sign_key, power_key, frac_key = jax.random.split(key, 3)
    sign = jax.random.randint(sign_key, (rows, cols), 0, 2).astype(jnp.float32) * 2.0 - 1.0
    power = jax.random.randint(power_key, (rows, cols), -2, 3).astype(jnp.float32)
    frac = jax.random.randint(frac_key, (rows, cols), 0, 8).astype(jnp.float32)
    return (sign * jnp.exp2(power) * (1.0 + frac / 8.0)).astype(jnp.bfloat16)


def draw_gate_codes(key, part):
    key = jax.random.fold_in(key, 11)
    return code_grid(key, D, FF)


def draw_up_codes(key, part):
    key = jax.random.fold_in(key, 23)
    return code_grid(key, D, FF)


def draw_down_codes(key, part):
    key = jax.random.fold_in(key, 37)
    return code_grid(key, FF, D)


def block_scale(rng, dims, shards, low, largest):
    factor_of, own = 1.0, jax.random.fold_in(rng, 6)
    for dim, shards_of in shards:
        heights = jnp.exp(jax.random.uniform(jax.random.fold_in(own, dim), (shards_of,), jnp.float32, low / len(shards), largest / len(shards)))
        factor_of = factor_of * jnp.repeat(heights, dims[dim] // shards_of).reshape([-1 if axis == dim else 1 for axis in range(len(dims))])
    return factor_of


def normal_values(key, extent, deviation, most, pieces=(), held_as=jnp.bfloat16):
    array = deviation * jax.random.normal(key, extent, jnp.float32)
    if pieces:
        array = array * block_scale(key, extent, pieces, -0.22, 0.18)
    return jnp.clip(array, -most, most).astype(held_as)


def setup_inputs(seed: int = 0) -> dict:
    key_list = jax.random.split(jax.random.key(seed), 9)
    tokens = normal_values(key_list[0], (TOKENS, D), 1.0, 6.0, ((0, 16), (1, 16)))
    grad_out = normal_values(key_list[1], (TOKENS, D), 1.0, 6.0, ((0, 16), (1, 16)))
    gate_codes = draw_gate_codes(jax.random.fold_in(key_list[8], 71), 0)
    gate_scale = jnp.clip(jnp.exp(math.log(0.008838835) - 1.3862944 * jax.random.uniform(key_list[3], (D // BLK, FF // BLK), jnp.float32) ** block_scale(key_list[3], (D // BLK, FF // BLK), ((0, 16), (1, 16)), -0.2, 0.2)), 0.0022097088, 0.008838835)
    up_codes = draw_up_codes(jax.random.fold_in(key_list[8], 71), 0)
    up_scale = jnp.clip(jnp.exp(math.log(0.008838835) - 1.3862944 * jax.random.uniform(key_list[5], (D // BLK, FF // BLK), jnp.float32) ** block_scale(key_list[5], (D // BLK, FF // BLK), ((0, 16), (1, 16)), -0.2, 0.2)), 0.0022097088, 0.008838835)
    down_codes = draw_down_codes(jax.random.fold_in(key_list[8], 71), 0)
    down_scale = jnp.clip(jnp.exp(math.log(0.006681531) - 1.3862944 * jax.random.uniform(key_list[7], (FF // BLK, D // BLK), jnp.float32) ** block_scale(key_list[7], (FF // BLK, D // BLK), ((0, 16), (1, 16)), -0.2, 0.2)), 0.0016703828, 0.006681531)
    return {"tokens": tokens, "grad_out": grad_out, "gate_codes": gate_codes, "gate_scale": gate_scale, "up_codes": up_codes, "up_scale": up_scale, "down_codes": down_codes, "down_scale": down_scale}


def dequant(codes, scales):
    expanded = jnp.repeat(jnp.repeat(scales, BLK, axis=0), BLK, axis=1)
    return (codes.astype(jnp.float32) * expanded).astype(jnp.bfloat16)


def block_squares(matrix):
    rows, cols = matrix.shape
    blocks = matrix.reshape(rows // BLK, BLK, cols // BLK, BLK)
    return jnp.sum(blocks * blocks, axis=(1, 3))


def contract_rows(left, right):
    return lax.dot_general(left, right, (((0,), (0,)), ((), ())), preferred_element_type=jnp.float32)


def contract_cols(left, right):
    return lax.dot_general(left, right, (((1,), (1,)), ((), ())), preferred_element_type=jnp.float32)


def width_parts(left, right):
    rows = left.shape[0]
    cols = right.shape[1]
    part = D // N_WID
    left_parts = left.astype(jnp.float32).reshape(rows, N_WID, part)
    right_parts = right.astype(jnp.float32).reshape(N_WID, part, cols)
    terms = jnp.einsum("tkd,kdw->ktw", left_parts, right_parts, precision=lax.Precision.HIGHEST)
    rounded = lax.optimization_barrier(terms.astype(jnp.bfloat16))
    return jnp.sum(rounded.astype(jnp.float32), axis=0)


def reference(tokens, grad_out, gate_codes, gate_scale, up_codes, up_scale, down_codes, down_scale):
    width = FF // N_HID
    sblock = width // BLK

    def step(grad_acc, index):
        start = index * width
        sstart = index * sblock
        gate_weight = dequant(lax.dynamic_slice_in_dim(gate_codes, start, width, 1),
                              lax.dynamic_slice_in_dim(gate_scale, sstart, sblock, 1))
        up_weight = dequant(lax.dynamic_slice_in_dim(up_codes, start, width, 1),
                            lax.dynamic_slice_in_dim(up_scale, sstart, sblock, 1))
        down_weight = dequant(lax.dynamic_slice_in_dim(down_codes, start, width, 0),
                              lax.dynamic_slice_in_dim(down_scale, sstart, sblock, 0))
        gate = width_parts(tokens, gate_weight)
        upper = width_parts(tokens, up_weight)
        grad_hidden = width_parts(grad_out, down_weight.T)
        sigma = jax.nn.sigmoid(gate)
        active = gate * sigma
        hidden = (active * upper).astype(jnp.bfloat16)
        d_gate = (grad_hidden * upper * sigma * (1.0 + gate * (1.0 - sigma))).astype(jnp.bfloat16)
        d_up = (grad_hidden * active).astype(jnp.bfloat16)
        term = contract_cols(d_gate, gate_weight) + contract_cols(d_up, up_weight)
        term_rounded = lax.optimization_barrier(term.astype(jnp.bfloat16))
        grad_acc = grad_acc + term_rounded.astype(jnp.float32)
        full_gate = contract_rows(tokens, d_gate)
        full_up = contract_rows(tokens, d_up)
        full_down = contract_rows(hidden, grad_out)
        norms = jnp.stack([block_squares(full_gate), block_squares(full_up), block_squares(full_down).T])
        return grad_acc, (full_gate.astype(jnp.bfloat16), full_up.astype(jnp.bfloat16),
                          full_down.astype(jnp.bfloat16), norms)

    start_acc = jnp.zeros((TOKENS, D), jnp.float32)
    grad_acc, stacked = lax.scan(step, start_acc, jnp.arange(N_HID, dtype=jnp.int32))
    pieces_gate, pieces_up, pieces_down, pieces_norm = stacked
    grad_gate = pieces_gate.transpose(1, 0, 2).reshape(D, FF)
    grad_up = pieces_up.transpose(1, 0, 2).reshape(D, FF)
    grad_down = pieces_down.reshape(FF, D)
    block_norms = pieces_norm.transpose(1, 2, 0, 3).reshape(3, D // BLK, FF // BLK)
    return grad_acc.astype(jnp.bfloat16), grad_gate, grad_up, grad_down, block_norms
```

```python
import functools

import jax
import jax.numpy as jnp
from jax import lax
from jax.experimental import pallas as pl
from jax.experimental.pallas import tpu as pltpu
from jax.sharding import PartitionSpec as P

BLK = 128
NZ = 8
CHUNKS = ((1, 7), (2, 6), (3, 5), (0, 4))
POS = {r: (c, h) for c, pair in enumerate(CHUNKS) for h, r in enumerate(pair)}
NC = len(CHUNKS)
ROWS = 16
ORDER = ((0, 1, 2), (1, 2, 0), (2, 0, 1))
BF = jnp.bfloat16
F32 = jnp.float32


def matmul(left, right, dims=((1,), (0,))):
    return lax.dot_general(left, right, (dims, ((), ())), preferred_element_type=F32)


def kernel(
    tok_in, gro_in, gc_in, gs, uc_in, us, dc_in, ds,
    gt_out, gg_out, gu_out, gd_out, bn_out,
    X, codes_g, codes_u, codes_d, wg, wu, wd, part, rb0, rb1, rb2, rb3, ag, term, zrecv, xsend, xrecv,
    st_g, st_u, st_d, st_t,
    loc_sem, own_sem, xs_sem, ring_s, ring_r, wid_s, wid_r, z_s, z_r, xf_sem, out_sem,
):
    hid, wid = lax.axis_index("hid"), lax.axis_index("wid")
    z, xhi = hid // 2, hid % 2
    y, xlo, core = wid // 4, (wid // 2) % 2, wid % 2
    bit_a, bit_b = (y + y // 2) % 2, y // 2
    bits = (xlo, bit_a, bit_b)
    core_peer = wid + 1 - 2 * core
    x_peer = (y * 2 + 1 - xlo) * 2 + core
    a_peer = ((y + 1 - 2 * (y % 2)) * 2 + xlo) * 2 + core
    b_peer = ((3 - y) * 2 + xlo) * 2 + core
    pair_peer = (x_peer, a_peer, b_peer)
    xhi_peer = z * 2 + 1 - xhi

    def z_peer(r):
        return ((z + r) % NZ) * 2 + xhi

    barrier = pltpu.get_barrier_semaphore()
    for peer in (core_peer,) + pair_peer:
        pl.semaphore_signal(barrier, inc=1, device_id={"wid": peer}, device_id_type=pl.DeviceIdType.MESH)
    for peer in [xhi_peer] + [z_peer(r) for r in range(1, NZ)]:
        pl.semaphore_signal(barrier, inc=1, device_id={"hid": peer}, device_id_type=pl.DeviceIdType.MESH)

    c0, h0 = POS[0]
    own = [
        pltpu.make_async_copy(tok_in, X.at[c0, 0, h0, 0], own_sem.at[0]),
        pltpu.make_async_copy(gro_in, X.at[c0, 1, h0, 0], own_sem.at[1]),
    ]
    loads = [
        pltpu.make_async_copy(gc_in, codes_g, loc_sem.at[0]),
        pltpu.make_async_copy(uc_in, codes_u, loc_sem.at[1]),
        pltpu.make_async_copy(dc_in, codes_d, loc_sem.at[2]),
    ]
    for copy in own + loads:
        copy.start()
    for copy in own:
        copy.wait()
    pl.semaphore_wait(barrier, 12)

    sends = []

    def remote(src, dst, send, recv, where):
        return pltpu.make_async_remote_copy(
            src_ref=src, dst_ref=dst, send_sem=send, recv_sem=recv,
            device_id=where, device_id_type=pl.DeviceIdType.MESH,
        )

    def go(copy):
        copy.start()
        sends.append(copy)

    x_copy = remote(X.at[c0, :, h0, 0], X.at[c0, :, h0, 1], xs_sem.at[0], xs_sem.at[1], {"hid": xhi_peer})
    ring = {}
    for way, sign in ((0, -1), (1, 1)):
        for j in range(1, 5):
            for xh in range(2):
                cs, hs = POS[(sign * (j - 1)) % NZ]
                cd, hd = POS[(sign * j) % NZ]
                kind = slice(None) if j < 4 else way
                ring[way, j, xh] = remote(
                    X.at[cs, kind, hs, xh], X.at[cd, kind, hd, xh],
                    ring_s.at[way, j - 1, xh], ring_r.at[way, j - 1, xh], {"hid": z_peer(-sign)},
                )

    def forward(j, xh):
        for way in range(2):
            ring[way, j, xh].wait_recv()
            if j < 4:
                go(ring[way, j + 1, xh])

    def dequant(codes, scales, weight):
        rows, cols = weight.shape
        for i in range(rows // BLK):
            for j in range(cols // BLK):
                at = (slice(i * BLK, (i + 1) * BLK), slice(j * BLK, (j + 1) * BLK))
                weight[at] = (codes[at].astype(F32) * scales[i, j]).astype(BF)

    go(x_copy)
    go(ring[0, 1, 0])
    go(ring[1, 1, 0])
    loads[0].wait()
    dequant(codes_g, gs, wg)
    forward(1, 0)
    x_copy.wait_recv()
    go(ring[0, 1, 1])
    go(ring[1, 1, 1])
    loads[1].wait()
    dequant(codes_u, us, wu)
    loads[2].wait()
    dequant(codes_d, ds, wd)
    forward(1, 1)

    def at_bits(free, other=None):
        index = []
        for d in range(3):
            if d in free:
                index.append(slice(None))
            elif d == other:
                index.append(1 - bits[d])
            else:
                index.append(bits[d])
        return tuple(index)

    def core_sum(c, k):
        return remote(part.at[c, k, 1 - core], rb0.at[c, k], wid_s.at[c, k, 0], wid_r.at[c, k, 0], {"wid": core_peer})

    def pair_sum(c, k, s):
        order = ORDER[k]
        index = at_bits(order[s:], order[s - 1])
        return remote(
            part.at[(c, k, core) + index], (rb1, rb2, rb3)[s - 1].at[c, k],
            wid_s.at[c, k, s], wid_r.at[c, k, s], {"wid": pair_peer[order[s - 1]]},
        )

    def pair_gather(c, k, s):
        order = ORDER[k]
        ref = ag.at[(c, k, core) + at_bits(order[s:])]
        return remote(ref, ref, wid_s.at[c, k, 7 - s], wid_r.at[c, k, 7 - s], {"wid": pair_peer[order[s - 1]]})

    def core_gather(c, k):
        ref = ag.at[c, k, core]
        return remote(ref, ref, wid_s.at[c, k, 7], wid_r.at[c, k, 7], {"wid": core_peer})

    def add_into(ref, other):
        ref[...] = (ref[...].astype(F32) + other[...].astype(F32)).astype(BF)

    def stage_partial(c):
        toks = X[c, 0].reshape(256, 512)
        part[c, 0] = matmul(toks, wg[...]).astype(BF).reshape(2, 2, 2, 2, ROWS, 896)
        go(core_sum(c, 0))
        part[c, 1] = matmul(toks, wu[...]).astype(BF).reshape(2, 2, 2, 2, ROWS, 896)
        go(core_sum(c, 1))
        grads = X[c, 1].reshape(256, 512)
        part[c, 2] = matmul(grads, wd[...], ((1,), (1,))).astype(BF).reshape(2, 2, 2, 2, ROWS, 896)
        go(core_sum(c, 2))

    def stage_core(c):
        for k in range(3):
            core_sum(c, k).wait_recv()
            add_into(part.at[c, k, core], rb0.at[c, k])
            go(pair_sum(c, k, 1))

    def stage_pair(c, s):
        for k in range(3):
            order = ORDER[k]
            pair_sum(c, k, s).wait_recv()
            add_into(part.at[(c, k, core) + at_bits(order[s:])], (rb1, rb2)[s - 1].at[c, k])
            go(pair_sum(c, k, s + 1))

    def stage_nonlinear(c):
        sums = []
        for k in range(3):
            pair_sum(c, k, 3).wait_recv()
            sums.append(part[(c, k, core) + bits].astype(F32) + rb3[c, k].astype(F32))
        gate, upper, grad = sums
        sigma = jax.nn.sigmoid(gate)
        active = gate * sigma
        ag[(c, 0, core) + bits] = (active * upper).astype(BF)
        go(pair_gather(c, 0, 3))
        ag[(c, 1, core) + bits] = (grad * upper * sigma * (1.0 + gate * (1.0 - sigma))).astype(BF)
        go(pair_gather(c, 1, 3))
        ag[(c, 2, core) + bits] = (grad * active).astype(BF)
        go(pair_gather(c, 2, 3))

    def stage_gather(c, s):
        for k in range(3):
            pair_gather(c, k, s).wait_recv()
            go(pair_gather(c, k, s - 1) if s > 1 else core_gather(c, k))

    def z_send(r):
        c, h = POS[r]
        back = (-r) % NZ
        return remote(term.at[c, h], zrecv.at[back], z_s.at[r], z_r.at[back], {"hid": z_peer(r)})

    def stage_term(c):
        for k in range(3):
            core_gather(c, k).wait_recv()
        total = matmul(ag[c, 1].reshape(256, 896), wg[...], ((1,), (1,)))
        total += matmul(ag[c, 2].reshape(256, 896), wu[...], ((1,), (1,)))
        term[c] = total.astype(BF).reshape(2, 128, 512)
        for r in CHUNKS[c]:
            if r:
                go(z_send(r))

    stages = [
        stage_partial,
        stage_core,
        lambda c: stage_pair(c, 1),
        lambda c: stage_pair(c, 2),
        stage_nonlinear,
        lambda c: stage_gather(c, 3),
        lambda c: stage_gather(c, 2),
        lambda c: stage_gather(c, 1),
        stage_term,
    ]
    forwards = [
        lambda: forward(2, 0),
        lambda: forward(2, 1),
        lambda: forward(3, 0),
        lambda: forward(3, 1),
        lambda: forward(4, 0),
        lambda: forward(4, 1),
    ]
    needs = (0, 2, 4, 6)
    done = 0
    stagger = 2
    for tick in range(len(stages) + stagger * (NC - 1)):
        for c in range(NC):
            step = tick - stagger * c
            if 0 <= step < len(stages):
                if step == 0:
                    while done < needs[c]:
                        forwards[done]()
                        done += 1
                stages[step](c)
        if done < len(forwards):
            forwards[done]()
            done += 1

    toks = X[:, 0].reshape(1024, 512)
    outs = []

    def block_sums(full):
        rows, cols = full.shape
        sums = jnp.sum((full * full).reshape(rows // BLK, BLK, cols), axis=1)
        of_block = (
            lax.broadcasted_iota(jnp.int32, (cols // BLK, cols), 1) // BLK
            == lax.broadcasted_iota(jnp.int32, (cols // BLK, cols), 0)
        ).astype(F32)
        return sums, of_block

    def exact(left, right):
        return lax.dot_general(
            left, right, (((1,), (1,)), ((), ())), precision=lax.Precision.HIGHEST, preferred_element_type=F32
        )

    def weight_grad(k, left, right, stage, out, flip):
        full = matmul(left, right, ((0,), (0,)))
        stage[...] = full.astype(BF)
        copy = pltpu.make_async_copy(stage, out, out_sem.at[k])
        copy.start()
        outs.append(copy)
        sums, of_block = block_sums(full)
        bn_out[k] = exact(of_block, sums) if flip else exact(sums, of_block)

    weight_grad(0, toks, ag[:, 1].reshape(1024, 896), st_g, gg_out, False)
    weight_grad(1, toks, ag[:, 2].reshape(1024, 896), st_u, gu_out, False)

    total = term[c0, h0].astype(F32)
    for r in (1, 7, 2, 6, 3, 5, 4):
        z_send((-r) % NZ).wait_recv()
        total += zrecv[r].astype(F32)
    xsend[...] = total[64:].astype(BF)
    last = remote(xsend, xrecv, xf_sem.at[0], xf_sem.at[1], {"hid": xhi_peer})
    go(last)
    weight_grad(2, ag[:, 0].reshape(1024, 896), X[:, 1].reshape(1024, 512), st_d, gd_out, True)
    last.wait_recv()
    st_t[...] = (total[:64] + xrecv[...].astype(F32)).astype(BF)
    copy = pltpu.make_async_copy(st_t, gt_out, out_sem.at[3])
    copy.start()
    outs.append(copy)
    for copy in outs:
        copy.wait()
    for copy in sends:
        copy.wait_send()


def body(tokens, grad_out, gate_codes, gate_scale, up_codes, up_scale, down_codes, down_scale):
    hbm = pl.BlockSpec(memory_space=pl.ANY)
    smem = pl.BlockSpec(memory_space=pltpu.SMEM)
    vmem = pl.BlockSpec(memory_space=pltpu.VMEM)
    dma = pltpu.SemaphoreType.DMA
    blocks = (ROWS, 896)
    return pl.pallas_call(
        kernel,
        out_shape=(
            jax.ShapeDtypeStruct((64, 512), BF),
            jax.ShapeDtypeStruct((512, 896), BF),
            jax.ShapeDtypeStruct((512, 896), BF),
            jax.ShapeDtypeStruct((896, 512), BF),
            jax.ShapeDtypeStruct((3, 4, 7), F32),
        ),
        in_specs=[hbm, hbm, hbm, smem, hbm, smem, hbm, smem],
        out_specs=(hbm, hbm, hbm, hbm, vmem),
        scratch_shapes=[
            pltpu.VMEM((NC, 2, 2, 2, 64, 512), BF),
            pltpu.VMEM((512, 896), BF),
            pltpu.VMEM((512, 896), BF),
            pltpu.VMEM((896, 512), BF),
            pltpu.VMEM((512, 896), BF),
            pltpu.VMEM((512, 896), BF),
            pltpu.VMEM((896, 512), BF),
            pltpu.VMEM((NC, 3, 2, 2, 2, 2) + blocks, BF),
            pltpu.VMEM((NC, 3, 2, 2, 2) + blocks, BF),
            pltpu.VMEM((NC, 3, 2, 2) + blocks, BF),
            pltpu.VMEM((NC, 3, 2) + blocks, BF),
            pltpu.VMEM((NC, 3) + blocks, BF),
            pltpu.VMEM((NC, 3, 2, 2, 2, 2) + blocks, BF),
            pltpu.VMEM((NC, 2, 128, 512), BF),
            pltpu.VMEM((NZ, 128, 512), BF),
            pltpu.VMEM((64, 512), BF),
            pltpu.VMEM((64, 512), BF),
            pltpu.VMEM((512, 896), BF),
            pltpu.VMEM((512, 896), BF),
            pltpu.VMEM((896, 512), BF),
            pltpu.VMEM((64, 512), BF),
            dma((3,)),
            dma((2,)),
            dma((2,)),
            dma((2, 4, 2)),
            dma((2, 4, 2)),
            dma((NC, 3, 8)),
            dma((NC, 3, 8)),
            dma((NZ,)),
            dma((NZ,)),
            dma((2,)),
            dma((4,)),
        ],
        compiler_params=pltpu.CompilerParams(
            collective_id=0, has_side_effects=True, vmem_limit_bytes=56 * 1024 * 1024
        ),
    )(tokens, grad_out, gate_codes, gate_scale, up_codes, up_scale, down_codes, down_scale)


def solution(mesh):
    in_specs = (
        P("hid", "wid"),
        P("hid", "wid"),
        P("wid", "hid"),
        P("wid", "hid"),
        P("wid", "hid"),
        P("wid", "hid"),
        P("hid", "wid"),
        P("hid", "wid"),
    )
    out_specs = (
        P("hid", "wid"),
        P("wid", "hid"),
        P("wid", "hid"),
        P("hid", "wid"),
        P(None, "wid", "hid"),
    )
    return jax.shard_map(body, mesh=mesh, in_specs=in_specs, out_specs=out_specs, check_vma=False)
```

```python
import jax
import jax.numpy as jnp
from jax import lax
from jax.experimental import pallas as pl
from jax.experimental.pallas import tpu as pltpu
from jax.sharding import PartitionSpec as P

BLK = 128
NZ = 8
CHUNKS = (((5, 0), (6, 1), (2, 1), (7, 1)), ((1, 1), (7, 0), (2, 0), (6, 0)), ((0, 0), (4, 1), (3, 1), (4, 0)), ((3, 0), (0, 1), (1, 0), (5, 1)))
CHAIN = ((2, 0), (2, 1), (4, 0), (4, 1))
STEPS = (
    ("Dq", 0), ("Dq", 1), ("Dq", 2), ("F", 1, 0, 0), ("Fx", 0), ("F", 1, 0, 1),
    ("Fx", 1), ("F", 2, 0, 0), ("F", 1, 1, 0), ("S", 1, 1), ("S", 1, 0), ("F", 2, 0, 1),
    ("C", 1, 1), ("C", 1, 0), ("F", 1, 1, 1), ("S", 1, 2), ("F", 3, 0, 0), ("C", 1, 2),
    ("F", 2, 1, 0), ("S", 0, 1), ("S", 0, 0), ("P1", 1, 1), ("P1", 1, 0), ("F", 3, 0, 1),
    ("C", 0, 1), ("C", 0, 0), ("F", 2, 1, 1), ("S", 0, 2), ("P1", 1, 2), ("F", 4, 0, 0),
    ("P2", 1, 0), ("C", 0, 2), ("P2", 1, 1), ("F", 3, 1, 0), ("F", 4, 0, 1), ("S", 3, 1),
    ("S", 3, 0), ("P1", 0, 0), ("P1", 0, 1), ("F", 3, 1, 1), ("S", 3, 2), ("C", 3, 1),
    ("C", 3, 0), ("P2", 1, 2), ("C", 3, 2), ("F", 4, 1, 0), ("S", 2, 0), ("S", 2, 1),
    ("P1", 0, 2), ("P2", 0, 0), ("F", 4, 1, 1), ("S", 2, 2), ("C", 2, 0), ("P2", 0, 1),
    ("C", 2, 1), ("C", 2, 2), ("P1", 3, 0), ("P1", 3, 1), ("N", 1), ("P1", 3, 2),
    ("P2", 0, 2), ("P1", 2, 1), ("P1", 2, 0), ("P1", 2, 2), ("P2", 3, 0), ("A3", 1, 1),
    ("A3", 1, 2), ("P2", 3, 1), ("N", 0), ("A3", 1, 0), ("P2", 3, 2), ("P2", 2, 0),
    ("P2", 2, 1), ("P2", 2, 2), ("A2", 1, 2), ("A3", 0, 2), ("A2", 1, 1), ("A3", 0, 0),
    ("A3", 0, 1), ("A2", 1, 0), ("N", 3), ("N", 2), ("A2", 0, 2), ("A1", 1, 2),
    ("A1", 1, 1), ("A2", 0, 1), ("A1", 1, 0), ("G", 1, 2), ("A3", 3, 0), ("T", 1),
    ("Z", 1, 2, 0), ("Z", 1, 6, 0), ("A3", 2, 1), ("A3", 2, 0), ("A3", 2, 2), ("A3", 3, 1),
    ("A3", 3, 2), ("A2", 0, 0), ("G", 1, 0), ("G", 1, 1), ("A1", 0, 2), ("A1", 0, 1),
    ("A2", 2, 1), ("Z", 1, 7, 0), ("A2", 2, 2), ("G", 0, 2), ("T", 0), ("Z", 0, 5, 0),
    ("Z", 0, 6, 1), ("Z", 0, 2, 1), ("A2", 3, 1), ("A2", 2, 0), ("A2", 3, 0), ("A2", 3, 2),
    ("G", 0, 1), ("A1", 0, 0), ("A1", 2, 1), ("A1", 2, 2), ("Z", 1, 1, 1), ("G", 0, 0),
    ("G", 2, 1), ("T", 2), ("Z", 2, 4, 1), ("Z", 2, 3, 1), ("Z", 2, 4, 0), ("A1", 2, 0),
    ("A1", 3, 2), ("A1", 3, 1), ("G", 2, 2), ("G", 2, 0), ("Z", 0, 7, 1), ("A1", 3, 0),
    ("T", 3), ("Z", 3, 1, 0), ("Z", 3, 5, 1), ("G", 3, 0), ("G", 3, 1), ("G", 3, 2),
    ("Z", 3, 3, 0), ("X",), ("E",),
)
POS = {block: (c, i) for c, blocks in enumerate(CHUNKS) for i, block in enumerate(blocks)}
NC = len(CHUNKS)
ROWS = 16
ORDER = ((0, 1, 2), (1, 2, 0), (2, 0, 1))
BF = jnp.bfloat16
F32 = jnp.float32


def matmul(left, right, dims=((1,), (0,))):
    return lax.dot_general(left, right, (dims, ((), ())), preferred_element_type=F32)


def far(block):
    return min(block[0], NZ - block[0])


def way_of(block):
    r, xh = block
    return 1 if r < 4 or (r == 4 and xh == 0) else -1


def chained(block):
    return (far(block), block[1]) in CHAIN


def feeder(block):
    r, xh = block
    before = ((r + way_of(block)) % NZ, xh)
    if r == 0 or r == 4 or not chained(before) or way_of(before) != way_of(block):
        return None
    return before


BLOCKS = [(r, xh) for r in range(1, NZ) for xh in range(2)]
HOME = [block for block in BLOCKS if far(block) == 1 or not chained(block)]
HOPS = sorted({1, NZ - 1} | {r for r, xh in BLOCKS if not chained((r, xh))})


def kernel(
    tok_in, gro_in, gc_in, gs, uc_in, us, dc_in, ds,
    gt_out, gg_out, gu_out, gd_out, bn_out,
    X, codes_g, codes_u, codes_d, wg, wu, wd, part, rb0, rb1, rb2, rb3, ag, term, zin, xsend, xrecv,
    acc_g, acc_u, acc_d,
    loc_sem, own_sem, xs_sem, ring_s, ring_r, wid_s, wid_r, z_s, z_r, xf_sem,
):
    hid, wid = lax.axis_index("hid"), lax.axis_index("wid")
    z, xhi = hid // 2, hid % 2
    y, xlo, core = wid // 4, (wid // 2) % 2, wid % 2
    bit_a, bit_b = (y + y // 2) % 2, y // 2
    bits = (xlo, bit_a, bit_b)
    core_peer = wid + 1 - 2 * core
    x_peer = (y * 2 + 1 - xlo) * 2 + core
    a_peer = ((y + 1 - 2 * (y % 2)) * 2 + xlo) * 2 + core
    b_peer = ((3 - y) * 2 + xlo) * 2 + core
    pair_peer = (x_peer, a_peer, b_peer)
    xhi_peer = z * 2 + 1 - xhi

    def z_peer(r):
        return ((z + r) % NZ) * 2 + xhi

    barrier = pltpu.get_barrier_semaphore()
    for peer in (core_peer,) + pair_peer:
        pl.semaphore_signal(barrier, inc=1, device_id={"wid": peer}, device_id_type=pl.DeviceIdType.MESH)
    for peer in [xhi_peer] + [z_peer(r) for r in sorted(set(HOPS) | {NZ - r for r in HOPS})]:
        pl.semaphore_signal(barrier, inc=1, device_id={"hid": peer}, device_id_type=pl.DeviceIdType.MESH)

    def rows(block, g):
        c, i = POS[block]
        return X.at[c, g, i]

    own = [
        pltpu.make_async_copy(tok_in, rows((0, 0), 0), own_sem.at[0]),
        pltpu.make_async_copy(gro_in, rows((0, 0), 1), own_sem.at[1]),
    ]
    loads = [
        pltpu.make_async_copy(gc_in, codes_g, loc_sem.at[0]),
        pltpu.make_async_copy(uc_in, codes_u, loc_sem.at[1]),
        pltpu.make_async_copy(dc_in, codes_d, loc_sem.at[2]),
    ]
    for copy in own + loads:
        copy.start()
    for copy in own:
        copy.wait()
    pl.semaphore_wait(barrier, 5 + len(set(HOPS) | {NZ - r for r in HOPS}))

    sends = []

    def remote(src, dst, send, recv, where):
        return pltpu.make_async_remote_copy(
            src_ref=src, dst_ref=dst, send_sem=send, recv_sem=recv,
            device_id=where, device_id_type=pl.DeviceIdType.MESH,
        )

    def go(copy):
        copy.start()
        sends.append(copy)

    x_copy = [
        remote(rows((0, 0), g), rows((0, 1), g), xs_sem.at[0, g], xs_sem.at[1, g], {"hid": xhi_peer}) for g in range(2)
    ]
    ring = {}
    for way, sign in ((0, -1), (1, 1)):
        for j in range(1, 5):
            for xh in range(2):
                for g in range(2):
                    if j < 4 or g == way:
                        ring[way, j, xh, g] = remote(
                            rows(((sign * (j - 1)) % NZ, xh), g), rows(((sign * j) % NZ, xh), g),
                            ring_s.at[way, j - 1, xh, g], ring_r.at[way, j - 1, xh, g], {"hid": z_peer(-sign)},
                        )

    def forward(j, xh, g):
        for way in range(2):
            if (way, j, xh, g) in ring:
                ring[way, j, xh, g].wait_recv()
                if (way, j + 1, xh, g) in ring:
                    go(ring[way, j + 1, xh, g])

    def forward_x(g):
        x_copy[g].wait_recv()
        for way in range(2):
            go(ring[way, 1, 1, g])

    def dequant(load, codes, scales, weight):
        load.wait()
        height, cols = weight.shape
        for i in range(height // BLK):
            for j in range(cols // BLK):
                at = (slice(i * BLK, (i + 1) * BLK), slice(j * BLK, (j + 1) * BLK))
                weight[at] = (codes[at].astype(F32) * scales(i, j)).astype(BF)

    for g in range(2):
        go(x_copy[g])
    for g in range(2):
        for way in range(2):
            go(ring[way, 1, 0, g])

    def at_bits(free, other=None):
        index = []
        for d in range(3):
            if d in free:
                index.append(slice(None))
            elif d == other:
                index.append(1 - bits[d])
            else:
                index.append(bits[d])
        return tuple(index)

    def core_sum(c, k):
        return remote(part.at[c, k, 1 - core], rb0.at[c, k], wid_s.at[c, k, 0], wid_r.at[c, k, 0], {"wid": core_peer})

    def pair_sum(c, k, s):
        order = ORDER[k]
        index = at_bits(order[s:], order[s - 1])
        return remote(
            part.at[(c, k, core) + index], (rb1, rb2, rb3)[s - 1].at[c, k],
            wid_s.at[c, k, s], wid_r.at[c, k, s], {"wid": pair_peer[order[s - 1]]},
        )

    def pair_gather(c, k, s):
        order = ORDER[k]
        ref = ag.at[(c, k, core) + at_bits(order[s:])]
        return remote(ref, ref, wid_s.at[c, k, 7 - s], wid_r.at[c, k, 7 - s], {"wid": pair_peer[order[s - 1]]})

    def core_gather(c, k):
        ref = ag.at[c, k, core]
        return remote(ref, ref, wid_s.at[c, k, 7], wid_r.at[c, k, 7], {"wid": core_peer})

    def add_into(ref, other):
        ref[...] = (ref[...].astype(F32) + other[...].astype(F32)).astype(BF)

    def step_partial(c, k):
        left = X[c, k // 2].reshape(256, 512)
        whole = matmul(left, wd[...], ((1,), (1,))) if k == 2 else matmul(left, (wg, wu)[k][...])
        part[c, k] = whole.astype(BF).reshape(2, 2, 2, 2, ROWS, 896)
        go(core_sum(c, k))

    def step_core(c, k):
        core_sum(c, k).wait_recv()
        add_into(part.at[c, k, core], rb0.at[c, k])
        go(pair_sum(c, k, 1))

    def step_pair(c, k, s):
        pair_sum(c, k, s).wait_recv()
        add_into(part.at[(c, k, core) + at_bits(ORDER[k][s:])], (rb1, rb2)[s - 1].at[c, k])
        go(pair_sum(c, k, s + 1))

    def step_nonlinear(c):
        sums = []
        for k in range(3):
            pair_sum(c, k, 3).wait_recv()
            sums.append(part[(c, k, core) + bits].astype(F32) + rb3[c, k].astype(F32))
        gate, upper, grad = sums
        sigma = jax.nn.sigmoid(gate)
        active = gate * sigma
        ag[(c, 1, core) + bits] = (grad * upper * sigma * (1.0 + gate * (1.0 - sigma))).astype(BF)
        go(pair_gather(c, 1, 3))
        ag[(c, 2, core) + bits] = (grad * active).astype(BF)
        go(pair_gather(c, 2, 3))
        ag[(c, 0, core) + bits] = (active * upper).astype(BF)
        go(pair_gather(c, 0, 3))

    def step_gather(c, k, s):
        pair_gather(c, k, s).wait_recv()
        go(pair_gather(c, k, s - 1) if s > 1 else core_gather(c, k))

    def z_send(block):
        r, xh = block
        c, i = POS[block]
        hop = way_of(block) % NZ if chained(block) else r
        return remote(term.at[c, i], zin.at[r, xh], z_s.at[r, xh], z_r.at[r, xh], {"hid": z_peer(hop)})

    landed = set()

    def landing(c, k):
        if (c, k) not in landed:
            landed.add((c, k))
            core_gather(c, k).wait_recv()
        return ag[c, k].reshape(256, 896)

    def step_term(c):
        total = matmul(landing(c, 1), wg[...], ((1,), (1,)))
        total += matmul(landing(c, 2), wu[...], ((1,), (1,)))
        term[c] = total.astype(BF).reshape(4, 64, 512)

    def step_home(c, r, xh):
        c, i = POS[r, xh]
        before = feeder((r, xh))
        if before is not None:
            z_send(before).wait_recv()
            add_into(term.at[c, i], zin.at[before])
        go(z_send((r, xh)))

    def home_sum(xh):
        total = term[POS[0, xh]].astype(F32)
        for block in HOME:
            if block[1] == xh:
                z_send(block).wait_recv()
                total += zin[block].astype(F32)
        return total

    last = remote(xsend, xrecv, xf_sem.at[0], xf_sem.at[1], {"hid": xhi_peer})

    def step_cross():
        xsend[...] = home_sum(1).astype(BF)
        go(last)

    def step_last():
        total = home_sum(0)
        last.wait_recv()
        gt_out[...] = (total + xrecv[...].astype(F32)).astype(BF)

    def block_sums(full):
        height, cols = full.shape
        sums = jnp.sum((full * full).reshape(height // BLK, BLK, cols), axis=1)
        of_block = (
            lax.broadcasted_iota(jnp.int32, (cols // BLK, cols), 1) // BLK
            == lax.broadcasted_iota(jnp.int32, (cols // BLK, cols), 0)
        ).astype(F32)
        return sums, of_block

    def exact(left, right):
        return lax.dot_general(
            left, right, (((1,), (1,)), ((), ())), precision=lax.Precision.HIGHEST, preferred_element_type=F32
        )

    seen = {0: 0, 1: 0, 2: 0}

    def step_grad(c, k):
        d = landing(c, k)
        if k == 0:
            full = matmul(d, X[c, 1].reshape(256, 512), ((0,), (0,)))
        else:
            full = matmul(X[c, 0].reshape(256, 512), d, ((0,), (0,)))
        acc = (acc_d, acc_g, acc_u)[k]
        if seen[k]:
            full += acc[...]
        seen[k] += 1
        if seen[k] < NC:
            acc[...] = full
            return
        out, row = ((gd_out, 2), (gg_out, 0), (gu_out, 1))[k]
        out[...] = full.astype(BF)
        sums, of_block = block_sums(full)
        bn_out[row] = exact(of_block, sums) if k == 0 else exact(sums, of_block)

    do = {
        "Dq": lambda k: dequant(
            loads[k],
            (codes_g, codes_u, codes_d)[k],
            (lambda i, j: gs[i, j], lambda i, j: us[i, j], lambda i, j: ds[j, i])[k],
            (wg, wu, wd)[k],
        ),
        "Fx": forward_x,
        "F": forward,
        "S": step_partial,
        "C": step_core,
        "P1": lambda c, k: step_pair(c, k, 1),
        "P2": lambda c, k: step_pair(c, k, 2),
        "N": step_nonlinear,
        "A3": lambda c, k: step_gather(c, k, 3),
        "A2": lambda c, k: step_gather(c, k, 2),
        "A1": lambda c, k: step_gather(c, k, 1),
        "T": step_term,
        "Z": step_home,
        "G": step_grad,
        "X": step_cross,
        "E": step_last,
    }
    for name, *at in STEPS:
        do[name](*at)
    for copy in sends:
        copy.wait_send()


def body(tokens, grad_out, gate_codes, gate_scale, up_codes, up_scale, down_codes, down_scale):
    hbm = pl.BlockSpec(memory_space=pl.ANY)
    smem = pl.BlockSpec(memory_space=pltpu.SMEM)
    vmem = pl.BlockSpec(memory_space=pltpu.VMEM)
    dma = pltpu.SemaphoreType.DMA
    blocks = (ROWS, 896)
    shapes = (
        jax.ShapeDtypeStruct((64, 512), BF),
        jax.ShapeDtypeStruct((512, 896), BF),
        jax.ShapeDtypeStruct((512, 896), BF),
        jax.ShapeDtypeStruct((896, 512), BF),
        jax.ShapeDtypeStruct((3, 4, 7), F32),
    )
    found = pl.pallas_call(
        kernel,
        out_shape=tuple(pltpu.VMEM(shape.shape, shape.dtype) for shape in shapes),
        in_specs=[hbm, hbm, hbm, smem, hbm, smem, hbm, smem],
        out_specs=(vmem,) * 5,
        scratch_shapes=[
            pltpu.VMEM((NC, 2, 4, 64, 512), BF),
            pltpu.VMEM((512, 896), BF),
            pltpu.VMEM((512, 896), BF),
            pltpu.VMEM((896, 512), BF),
            pltpu.VMEM((512, 896), BF),
            pltpu.VMEM((512, 896), BF),
            pltpu.VMEM((896, 512), BF),
            pltpu.VMEM((NC, 3, 2, 2, 2, 2) + blocks, BF),
            pltpu.VMEM((NC, 3, 2, 2, 2) + blocks, BF),
            pltpu.VMEM((NC, 3, 2, 2) + blocks, BF),
            pltpu.VMEM((NC, 3, 2) + blocks, BF),
            pltpu.VMEM((NC, 3) + blocks, BF),
            pltpu.VMEM((NC, 3, 2, 2, 2, 2) + blocks, BF),
            pltpu.VMEM((NC, 4, 64, 512), BF),
            pltpu.VMEM((NZ, 2, 64, 512), BF),
            pltpu.VMEM((64, 512), BF),
            pltpu.VMEM((64, 512), BF),
            pltpu.VMEM((512, 896), F32),
            pltpu.VMEM((512, 896), F32),
            pltpu.VMEM((896, 512), F32),
            dma((3,)),
            dma((2,)),
            dma((2, 2)),
            dma((2, 4, 2, 2)),
            dma((2, 4, 2, 2)),
            dma((NC, 3, 8)),
            dma((NC, 3, 8)),
            dma((NZ, 2)),
            dma((NZ, 2)),
            dma((2,)),
        ],
        compiler_params=pltpu.CompilerParams(
            collective_id=0, has_side_effects=True, vmem_limit_bytes=60 * 1024 * 1024
        ),
    )(tokens, grad_out, gate_codes, gate_scale, up_codes, up_scale, down_codes, down_scale.T)
    return found


def solution(mesh):
    in_specs = (
        P("hid", "wid"),
        P("hid", "wid"),
        P("wid", "hid"),
        P("wid", "hid"),
        P("wid", "hid"),
        P("wid", "hid"),
        P("hid", "wid"),
        P("hid", "wid"),
    )
    out_specs = (
        P("hid", "wid"),
        P("wid", "hid"),
        P("wid", "hid"),
        P("hid", "wid"),
        P(None, "wid", "hid"),
    )
    return jax.shard_map(body, mesh=mesh, in_specs=in_specs, out_specs=out_specs, check_vma=False)
```

```python
import jax
import jax.numpy as jnp
from jax import lax
from jax.experimental import pallas as pl
from jax.experimental.pallas import tpu as pltpu
from jax.sharding import PartitionSpec as P

BLK = 128
NZ = 8
CHUNKS = (((2, 0), (7, 0), (0, 1), (6, 0)), ((1, 1), (1, 0), (0, 0), (5, 0)), ((3, 1), (7, 1), (5, 1), (4, 1)), ((2, 1), (6, 1), (4, 0), (3, 0)))
CHAIN = ((2, 0), (2, 1), (3, 1), (4, 0), (4, 1))
DIRECT = ((1, 1), (2, 1), (5, 1), (7, 1))
ACROSS = (1,)
SPREAD = (2,)
STEPS = (
    ("Dq", 0), ("Dq", 1), ("Dq", 2), ("F", 1, 0, 0), ("Fx", 0), ("F", 1, 0, 1),
    ("Fx", 1), ("F", 2, 0, 0), ("S", 0, 1), ("S", 0, 0), ("F", 2, 0, 1), ("S", 0, 2),
    ("F", 1, 1, 0), ("C", 0, 1), ("C", 0, 0), ("C", 0, 2), ("F", 3, 0, 0), ("S", 1, 1),
    ("S", 1, 0), ("F", 1, 1, 1), ("F", 3, 0, 1), ("S", 1, 2), ("C", 1, 1), ("C", 1, 0),
    ("F", 2, 1, 0), ("P1", 0, 1), ("C", 1, 2), ("P1", 0, 0), ("F", 4, 0, 0), ("S", 3, 1),
    ("S", 3, 0), ("P1", 0, 2), ("F", 2, 1, 1), ("C", 3, 1), ("F", 4, 0, 1), ("S", 3, 2),
    ("C", 3, 0), ("P2", 0, 1), ("P1", 1, 0), ("P1", 1, 1), ("F", 3, 1, 0), ("P2", 0, 0),
    ("C", 3, 2), ("P2", 0, 2), ("P1", 1, 2), ("F", 3, 1, 1), ("P2", 1, 1), ("P1", 3, 1),
    ("F", 4, 1, 0), ("S", 2, 1), ("S", 2, 0), ("P1", 3, 0), ("P2", 1, 0), ("N", 0),
    ("F", 4, 1, 1), ("P2", 1, 2), ("S", 2, 2), ("C", 2, 0), ("C", 2, 1), ("P1", 3, 2),
    ("P2", 3, 1), ("C", 2, 2), ("P2", 3, 0), ("A3", 0, 1), ("A3", 0, 2), ("A3", 0, 0),
    ("N", 1), ("P1", 2, 0), ("P1", 2, 1), ("P2", 3, 2), ("P1", 2, 2), ("A2", 0, 0),
    ("A3", 1, 2), ("A2", 0, 2), ("A2", 0, 1), ("A3", 1, 1), ("A3", 1, 0), ("N", 3),
    ("N", 2), ("A1", 0, 1), ("A1", 0, 0), ("A1", 0, 2), ("A2", 1, 0), ("G", 0, 1),
    ("A2", 1, 1), ("A2", 1, 2), ("A3", 3, 2), ("G", 0, 0), ("A3", 3, 1), ("A3", 3, 0),
    ("T", 0), ("Z", 0, 2, 0), ("Z", 0, 6, 0), ("X",), ("G", 0, 2), ("A2", 2, 0),
    ("A2", 2, 2), ("A2", 2, 1), ("A1", 1, 1), ("Z", 0, 7, 0), ("A1", 1, 0), ("A1", 1, 2),
    ("A2", 3, 0), ("G", 1, 1), ("A2", 3, 1), ("A2", 3, 2), ("G", 1, 0), ("T", 1),
    ("Z", 1, 1, 1), ("Z", 1, 1, 0), ("Z", 1, 5, 0), ("A1", 2, 1), ("G", 1, 2), ("A1", 2, 2),
    ("G", 2, 1), ("A1", 2, 0), ("T", 2), ("Z", 2, 3, 1), ("Z", 2, 4, 1), ("A1", 3, 1),
    ("A1", 3, 2), ("G", 2, 2), ("G", 2, 0), ("A1", 3, 0), ("T", 3), ("Z", 3, 6, 1),
    ("Z", 3, 4, 0), ("G", 3, 0), ("Z", 3, 2, 1), ("G", 3, 1), ("G", 3, 2), ("Z", 2, 5, 1),
    ("Z", 2, 7, 1), ("Z", 3, 3, 0), ("E",),
)
POS = {block: (c, i) for c, blocks in enumerate(CHUNKS) for i, block in enumerate(blocks)}
NC = len(CHUNKS)
ROWS = 16
ORDER = ((0, 1, 2), (1, 2, 0), (2, 0, 1))
BF = jnp.bfloat16
F32 = jnp.float32


def matmul(left, right, dims=((1,), (0,))):
    return lax.dot_general(left, right, (dims, ((), ())), preferred_element_type=F32)


def far(block):
    return min(block[0], NZ - block[0])


def way_of(block):
    r, xh = block
    return 1 if r < 4 or (r == 4 and xh == 0) else -1


def chained(block):
    return (far(block), block[1]) in CHAIN and block not in DIRECT


def feeder(block):
    r, xh = block
    before = ((r + way_of(block)) % NZ, xh)
    if r == 0 or r == 4 or not chained(before) or way_of(before) != way_of(block):
        return None
    return before


BLOCKS = [(r, xh) for r in range(1, NZ) for xh in range(2)]
HOME = [block for block in BLOCKS if far(block) == 1 or not chained(block)]
HOPS = {1, NZ - 1} | {r for r, xh in BLOCKS if not chained((r, xh)) and (r, xh) not in DIRECT}
HOPS = sorted(HOPS | {NZ - r for r in HOPS})
SIDE = sorted({r for r, _ in DIRECT} | {NZ - r for r, _ in DIRECT})


def kernel(
    tok_in, gro_in, gc_in, gs, uc_in, us, dc_in, ds,
    gt_out, gg_out, gu_out, gd_out, bn_out,
    X, codes_g, codes_u, codes_d, wg, wu, wd, part, rb0, rb1, rb2, rb3, ag, term, zin, xsend, xrecv,
    acc_g, acc_u, acc_d,
    loc_sem, own_sem, xs_sem, ring_s, ring_r, side_s, side_r, wid_s, wid_r, z_s, z_r, xf_sem,
):
    hid, wid = lax.axis_index("hid"), lax.axis_index("wid")
    z, xhi = hid // 2, hid % 2
    y, xlo, core = wid // 4, (wid // 2) % 2, wid % 2
    bit_a, bit_b = (y + y // 2) % 2, y // 2
    bits = (xlo, bit_a, bit_b)
    core_peer = wid + 1 - 2 * core

    def flipped(dims):
        row = (y, y + 1 - 2 * (y % 2), 3 - y, (y + 2) % 4)[(1 in dims) + 2 * (2 in dims)]
        return (row * 2 + (1 - xlo if 0 in dims else xlo)) * 2 + core

    pair_peer = tuple(flipped((d,)) for d in range(3))
    xhi_peer = z * 2 + 1 - xhi

    def z_peer(r):
        return ((z + r) % NZ) * 2 + xhi

    def side_peer(r):
        return ((z + r) % NZ) * 2 + 1 - xhi

    barrier = pltpu.get_barrier_semaphore()
    near = (core_peer,) + pair_peer
    if SPREAD:
        near += tuple(flipped(order[1:]) for order in ORDER)
    across = [xhi_peer] + [z_peer(r) for r in HOPS] + [side_peer(r) for r in SIDE]
    for peer in near:
        pl.semaphore_signal(barrier, inc=1, device_id={"wid": peer}, device_id_type=pl.DeviceIdType.MESH)
    for peer in across:
        pl.semaphore_signal(barrier, inc=1, device_id={"hid": peer}, device_id_type=pl.DeviceIdType.MESH)

    def rows(block, g):
        c, i = POS[block]
        return X.at[c, g, i]

    own = [
        pltpu.make_async_copy(tok_in, rows((0, 0), 0), own_sem.at[0]),
        pltpu.make_async_copy(gro_in, rows((0, 0), 1), own_sem.at[1]),
    ]
    loads = [
        pltpu.make_async_copy(gc_in, codes_g, loc_sem.at[0]),
        pltpu.make_async_copy(uc_in, codes_u, loc_sem.at[1]),
        pltpu.make_async_copy(dc_in, codes_d, loc_sem.at[2]),
    ]
    for copy in own + loads:
        copy.start()
    for copy in own:
        copy.wait()
    pl.semaphore_wait(barrier, len(near) + len(across))

    sends = []

    def remote(src, dst, send, recv, where):
        return pltpu.make_async_remote_copy(
            src_ref=src, dst_ref=dst, send_sem=send, recv_sem=recv,
            device_id=where, device_id_type=pl.DeviceIdType.MESH,
        )

    def go(copy):
        copy.start()
        sends.append(copy)

    x_copy = [
        remote(rows((0, 0), g), rows((0, 1), g), xs_sem.at[0, g], xs_sem.at[1, g], {"hid": xhi_peer}) for g in range(2)
    ]
    ring = {}
    for way, sign in ((0, -1), (1, 1)):
        for j in range(1, 5):
            for xh in range(2):
                for g in range(2):
                    if (j < 4 or g == way) and not (xh == 1 and j in ACROSS):
                        ring[way, j, xh, g] = remote(
                            rows(((sign * (j - 1)) % NZ, xh), g), rows(((sign * j) % NZ, xh), g),
                            ring_s.at[way, j - 1, xh, g], ring_r.at[way, j - 1, xh, g], {"hid": z_peer(-sign)},
                        )

    side = {}
    for way, sign in ((0, -1), (1, 1)):
        for j in ACROSS:
            for g in range(2):
                if j < 4 or g == way:
                    side[way, j, g] = remote(
                        rows(((sign * j) % NZ, 0), g), rows(((sign * j) % NZ, 1), g),
                        side_s.at[way, j - 1, g], side_r.at[way, j - 1, g], {"hid": xhi_peer},
                    )

    def forward(j, xh, g):
        for way in range(2):
            came = side.get((way, j, g)) if xh == 1 and j in ACROSS else ring.get((way, j, xh, g))
            if came is not None:
                came.wait_recv()
        for way in range(2):
            if (way, j + 1, xh, g) in ring:
                go(ring[way, j + 1, xh, g])
        for way in range(2):
            if xh == 0 and (way, j, g) in side:
                go(side[way, j, g])

    def forward_x(g):
        x_copy[g].wait_recv()
        for way in range(2):
            if (way, 1, 1, g) in ring:
                go(ring[way, 1, 1, g])

    def dequant(load, codes, scales, weight):
        load.wait()
        height, cols = weight.shape
        for i in range(height // BLK):
            for j in range(cols // BLK):
                at = (slice(i * BLK, (i + 1) * BLK), slice(j * BLK, (j + 1) * BLK))
                weight[at] = (codes[at].astype(F32) * scales(i, j)).astype(BF)

    for g in range(2):
        go(x_copy[g])
    for g in range(2):
        for way in range(2):
            go(ring[way, 1, 0, g])

    def at_bits(free, other=None):
        index = []
        for d in range(3):
            if d in free:
                index.append(slice(None))
            elif d == other:
                index.append(1 - bits[d])
            else:
                index.append(bits[d])
        return tuple(index)

    def core_sum(c, k):
        return remote(part.at[c, k, 1 - core], rb0.at[c, k], wid_s.at[c, k, 0], wid_r.at[c, k, 0], {"wid": core_peer})

    def pair_sum(c, k, s):
        order = ORDER[k]
        index = at_bits(order[s:], order[s - 1])
        return remote(
            part.at[(c, k, core) + index], (rb1, rb2, rb3)[s - 1].at[c, k],
            wid_s.at[c, k, s], wid_r.at[c, k, s], {"wid": pair_peer[order[s - 1]]},
        )

    def pair_gather(c, k, s):
        order = ORDER[k]
        ref = ag.at[(c, k, core) + at_bits(order[s:])]
        return remote(ref, ref, wid_s.at[c, k, 7 - s], wid_r.at[c, k, 7 - s], {"wid": pair_peer[order[s - 1]]})

    def core_gather(c, k):
        ref = ag.at[c, k, core]
        return remote(ref, ref, wid_s.at[c, k, 7], wid_r.at[c, k, 7], {"wid": core_peer})

    def spread(k, i):
        return ((ORDER[k][1],), (ORDER[k][2],), ORDER[k][1:])[i]

    def spread_sum(c, k, i):
        crossed = spread(k, i)
        index = tuple(1 - bits[d] if d in crossed else bits[d] for d in range(3))
        sem = (2, 3, 8)[i]
        return remote(
            part.at[(c, k, core) + index], spread_slot(c, k, i),
            wid_s.at[c, k, sem], wid_r.at[c, k, sem], {"wid": flipped(crossed)},
        )

    def spread_slot(c, k, i):
        return rb3.at[c, k] if i == 2 else rb2.at[c, k, i]

    def spread_gather(c, k, i):
        ref = ag.at[(c, k, core) + bits]
        sem = (4, 5, 9)[i]
        return remote(ref, ref, wid_s.at[c, k, sem], wid_r.at[c, k, sem], {"wid": flipped(spread(k, i))})

    def add_into(ref, other):
        ref[...] = (ref[...].astype(F32) + other[...].astype(F32)).astype(BF)

    def step_partial(c, k):
        left = X[c, k // 2].reshape(256, 512)
        whole = matmul(left, wd[...], ((1,), (1,))) if k == 2 else matmul(left, (wg, wu)[k][...])
        part[c, k] = whole.astype(BF).reshape(2, 2, 2, 2, ROWS, 896)
        go(core_sum(c, k))

    def step_core(c, k):
        core_sum(c, k).wait_recv()
        add_into(part.at[c, k, core], rb0.at[c, k])
        go(pair_sum(c, k, 1))

    def step_pair(c, k, s):
        pair_sum(c, k, s).wait_recv()
        add_into(part.at[(c, k, core) + at_bits(ORDER[k][s:])], (rb1, rb2)[s - 1].at[c, k])
        if c in SPREAD:
            for i in range(3):
                go(spread_sum(c, k, i))
        else:
            go(pair_sum(c, k, s + 1))

    def step_nonlinear(c):
        sums = []
        for k in range(3):
            total = part[(c, k, core) + bits].astype(F32)
            if c in SPREAD:
                for i in range(3):
                    spread_sum(c, k, i).wait_recv()
                    total += spread_slot(c, k, i)[...].astype(F32)
            else:
                pair_sum(c, k, 3).wait_recv()
                total += rb3[c, k].astype(F32)
            sums.append(total)

        def pass_on(k):
            if c in SPREAD:
                for i in range(3):
                    go(spread_gather(c, k, i))
            else:
                go(pair_gather(c, k, 3))

        gate, upper, grad = sums
        sigma = jax.nn.sigmoid(gate)
        active = gate * sigma
        ag[(c, 1, core) + bits] = (grad * upper * sigma * (1.0 + gate * (1.0 - sigma))).astype(BF)
        pass_on(1)
        ag[(c, 2, core) + bits] = (grad * active).astype(BF)
        pass_on(2)
        ag[(c, 0, core) + bits] = (active * upper).astype(BF)
        pass_on(0)

    def step_gather(c, k, s):
        if c in SPREAD and s == 2:
            for i in range(3):
                spread_gather(c, k, i).wait_recv()
        else:
            pair_gather(c, k, s).wait_recv()
        go(pair_gather(c, k, s - 1) if s > 1 else core_gather(c, k))

    def z_send(block):
        r, xh = block
        c, i = POS[block]
        if block in DIRECT:
            peer = side_peer(r)
        else:
            peer = z_peer(way_of(block) % NZ if chained(block) else r)
        return remote(term.at[c, i], zin.at[r, xh], z_s.at[r, xh], z_r.at[r, xh], {"hid": peer})

    landed = set()

    def landing(c, k):
        if (c, k) not in landed:
            landed.add((c, k))
            core_gather(c, k).wait_recv()
        return ag[c, k].reshape(256, 896)

    def step_term(c):
        total = matmul(landing(c, 1), wg[...], ((1,), (1,)))
        total += matmul(landing(c, 2), wu[...], ((1,), (1,)))
        term[c] = total.astype(BF).reshape(4, 64, 512)

    def step_home(c, r, xh):
        c, i = POS[r, xh]
        before = feeder((r, xh))
        if before is not None:
            z_send(before).wait_recv()
            add_into(term.at[c, i], zin.at[before])
        go(z_send((r, xh)))

    def home_sum(xh):
        total = term[POS[0, xh]].astype(F32)
        for block in HOME:
            if (0 if block in DIRECT else block[1]) == xh:
                z_send(block).wait_recv()
                total += zin[block].astype(F32)
        return total

    last = remote(xsend, xrecv, xf_sem.at[0], xf_sem.at[1], {"hid": xhi_peer})

    def step_cross():
        xsend[...] = home_sum(1).astype(BF)
        go(last)

    def step_last():
        total = home_sum(0)
        last.wait_recv()
        gt_out[...] = (total + xrecv[...].astype(F32)).astype(BF)

    def block_sums(full):
        height, cols = full.shape
        sums = jnp.sum((full * full).reshape(height // BLK, BLK, cols), axis=1)
        of_block = (
            lax.broadcasted_iota(jnp.int32, (cols // BLK, cols), 1) // BLK
            == lax.broadcasted_iota(jnp.int32, (cols // BLK, cols), 0)
        ).astype(F32)
        return sums, of_block

    def exact(left, right):
        return lax.dot_general(
            left, right, (((1,), (1,)), ((), ())), precision=lax.Precision.HIGHEST, preferred_element_type=F32
        )

    seen = {0: 0, 1: 0, 2: 0}

    def step_grad(c, k):
        d = landing(c, k)
        if k == 0:
            full = matmul(d, X[c, 1].reshape(256, 512), ((0,), (0,)))
        else:
            full = matmul(X[c, 0].reshape(256, 512), d, ((0,), (0,)))
        acc = (acc_d, acc_g, acc_u)[k]
        if seen[k]:
            full += acc[...]
        seen[k] += 1
        if seen[k] < NC:
            acc[...] = full
            return
        out, row = ((gd_out, 2), (gg_out, 0), (gu_out, 1))[k]
        out[...] = full.astype(BF)
        sums, of_block = block_sums(full)
        bn_out[row] = exact(of_block, sums) if k == 0 else exact(sums, of_block)

    do = {
        "Dq": lambda k: dequant(
            loads[k],
            (codes_g, codes_u, codes_d)[k],
            (lambda i, j: gs[i, j], lambda i, j: us[i, j], lambda i, j: ds[j, i])[k],
            (wg, wu, wd)[k],
        ),
        "Fx": forward_x,
        "F": forward,
        "S": step_partial,
        "C": step_core,
        "P1": lambda c, k: step_pair(c, k, 1),
        "P2": lambda c, k: step_pair(c, k, 2),
        "N": step_nonlinear,
        "A3": lambda c, k: step_gather(c, k, 3),
        "A2": lambda c, k: step_gather(c, k, 2),
        "A1": lambda c, k: step_gather(c, k, 1),
        "T": step_term,
        "Z": step_home,
        "G": step_grad,
        "X": step_cross,
        "E": step_last,
    }
    for name, *at in STEPS:
        do[name](*at)
    for copy in sends:
        copy.wait_send()


def body(tokens, grad_out, gate_codes, gate_scale, up_codes, up_scale, down_codes, down_scale):
    hbm = pl.BlockSpec(memory_space=pl.ANY)
    smem = pl.BlockSpec(memory_space=pltpu.SMEM)
    vmem = pl.BlockSpec(memory_space=pltpu.VMEM)
    dma = pltpu.SemaphoreType.DMA
    blocks = (ROWS, 896)
    shapes = (
        jax.ShapeDtypeStruct((64, 512), BF),
        jax.ShapeDtypeStruct((512, 896), BF),
        jax.ShapeDtypeStruct((512, 896), BF),
        jax.ShapeDtypeStruct((896, 512), BF),
        jax.ShapeDtypeStruct((3, 4, 7), F32),
    )
    found = pl.pallas_call(
        kernel,
        out_shape=tuple(pltpu.VMEM(shape.shape, shape.dtype) for shape in shapes),
        in_specs=[hbm, hbm, hbm, smem, hbm, smem, hbm, smem],
        out_specs=(vmem,) * 5,
        scratch_shapes=[
            pltpu.VMEM((NC, 2, 4, 64, 512), BF),
            pltpu.VMEM((512, 896), BF),
            pltpu.VMEM((512, 896), BF),
            pltpu.VMEM((896, 512), BF),
            pltpu.VMEM((512, 896), BF),
            pltpu.VMEM((512, 896), BF),
            pltpu.VMEM((896, 512), BF),
            pltpu.VMEM((NC, 3, 2, 2, 2, 2) + blocks, BF),
            pltpu.VMEM((NC, 3, 2, 2, 2) + blocks, BF),
            pltpu.VMEM((NC, 3, 2, 2) + blocks, BF),
            pltpu.VMEM((NC, 3, 2) + blocks, BF),
            pltpu.VMEM((NC, 3) + blocks, BF),
            pltpu.VMEM((NC, 3, 2, 2, 2, 2) + blocks, BF),
            pltpu.VMEM((NC, 4, 64, 512), BF),
            pltpu.VMEM((NZ, 2, 64, 512), BF),
            pltpu.VMEM((64, 512), BF),
            pltpu.VMEM((64, 512), BF),
            pltpu.VMEM((512, 896), F32),
            pltpu.VMEM((512, 896), F32),
            pltpu.VMEM((896, 512), F32),
            dma((3,)),
            dma((2,)),
            dma((2, 2)),
            dma((2, 4, 2, 2)),
            dma((2, 4, 2, 2)),
            dma((2, 4, 2)),
            dma((2, 4, 2)),
            dma((NC, 3, 10)),
            dma((NC, 3, 10)),
            dma((NZ, 2)),
            dma((NZ, 2)),
            dma((2,)),
        ],
        compiler_params=pltpu.CompilerParams(
            collective_id=0, has_side_effects=True, vmem_limit_bytes=60 * 1024 * 1024
        ),
    )(tokens, grad_out, gate_codes, gate_scale, up_codes, up_scale, down_codes, down_scale.T)
    return found


def solution(mesh):
    in_specs = (
        P("hid", "wid"),
        P("hid", "wid"),
        P("wid", "hid"),
        P("wid", "hid"),
        P("wid", "hid"),
        P("wid", "hid"),
        P("hid", "wid"),
        P("hid", "wid"),
    )
    out_specs = (
        P("hid", "wid"),
        P("wid", "hid"),
        P("wid", "hid"),
        P("hid", "wid"),
        P(None, "wid", "hid"),
    )
    return jax.shard_map(body, mesh=mesh, in_specs=in_specs, out_specs=out_specs, check_vma=False)
```

```python
import jax
import jax.numpy as jnp
from jax import lax
from jax.experimental import pallas as pl
from jax.experimental.pallas import tpu as pltpu
from jax.sharding import PartitionSpec as P

BLK = 128
NZ = 8
CHUNKS = (((2, 0), (7, 0), (0, 1), (6, 0)), ((1, 1), (1, 0), (0, 0), (5, 0)), ((3, 1), (7, 1), (5, 1), (4, 1)), ((2, 1), (6, 1), (4, 0), (3, 0)))
CHAIN = ((2, 0), (2, 1), (3, 1), (4, 0), (4, 1))
DIRECT = ((1, 1), (2, 1), (5, 1), (7, 1))
ACROSS = (1,)
SPREAD = (2,)
STEPS = (
    ("Dq", 0), ("Dq", 1), ("Dq", 2), ("F", 1, 0, 0), ("Fx", 0), ("F", 1, 0, 1),
    ("Fx", 1), ("F", 2, 0, 0), ("S", 0, 1), ("S", 0, 0), ("F", 2, 0, 1), ("S", 0, 2),
    ("F", 1, 1, 0), ("C", 0, 1), ("C", 0, 0), ("C", 0, 2), ("F", 3, 0, 0), ("S", 1, 1),
    ("S", 1, 0), ("F", 1, 1, 1), ("F", 3, 0, 1), ("S", 1, 2), ("C", 1, 1), ("C", 1, 0),
    ("F", 2, 1, 0), ("P1", 0, 1), ("C", 1, 2), ("P1", 0, 0), ("F", 4, 0, 0), ("S", 3, 1),
    ("S", 3, 0), ("P1", 0, 2), ("F", 2, 1, 1), ("C", 3, 1), ("F", 4, 0, 1), ("S", 3, 2),
    ("C", 3, 0), ("P2", 0, 1), ("P1", 1, 0), ("P1", 1, 1), ("F", 3, 1, 0), ("P2", 0, 0),
    ("C", 3, 2), ("P2", 0, 2), ("P1", 1, 2), ("F", 3, 1, 1), ("P2", 1, 1), ("P1", 3, 1),
    ("F", 4, 1, 0), ("S", 2, 1), ("S", 2, 0), ("P1", 3, 0), ("P2", 1, 0), ("N", 0),
    ("F", 4, 1, 1), ("P2", 1, 2), ("S", 2, 2), ("C", 2, 0), ("C", 2, 1), ("P1", 3, 2),
    ("P2", 3, 1), ("C", 2, 2), ("P2", 3, 0), ("A3", 0, 1), ("A3", 0, 2), ("A3", 0, 0),
    ("N", 1), ("P1", 2, 0), ("P1", 2, 1), ("P2", 3, 2), ("P1", 2, 2), ("A2", 0, 0),
    ("A3", 1, 2), ("A2", 0, 2), ("A2", 0, 1), ("A3", 1, 1), ("A3", 1, 0), ("N", 3),
    ("N", 2), ("A1", 0, 1), ("A1", 0, 0), ("A1", 0, 2), ("A2", 1, 0), ("G", 0, 1),
    ("A2", 1, 1), ("A2", 1, 2), ("A3", 3, 2), ("G", 0, 0), ("A3", 3, 1), ("A3", 3, 0),
    ("T", 0), ("Z", 0, 2, 0), ("Z", 0, 6, 0), ("X",), ("G", 0, 2), ("A2", 2, 0),
    ("A2", 2, 2), ("A2", 2, 1), ("A1", 1, 1), ("Z", 0, 7, 0), ("A1", 1, 0), ("A1", 1, 2),
    ("A2", 3, 0), ("G", 1, 1), ("A2", 3, 1), ("A2", 3, 2), ("G", 1, 0), ("T", 1),
    ("Z", 1, 1, 1), ("Z", 1, 1, 0), ("Z", 1, 5, 0), ("A1", 2, 1), ("G", 1, 2), ("A1", 2, 2),
    ("G", 2, 1), ("A1", 2, 0), ("T", 2), ("Z", 2, 3, 1), ("Z", 2, 4, 1), ("A1", 3, 1),
    ("A1", 3, 2), ("G", 2, 2), ("G", 2, 0), ("A1", 3, 0), ("T", 3), ("Z", 3, 6, 1),
    ("Z", 3, 4, 0), ("G", 3, 0), ("Z", 3, 2, 1), ("G", 3, 1), ("G", 3, 2), ("Z", 2, 5, 1),
    ("Z", 2, 7, 1), ("Z", 3, 3, 0), ("E",),
)
POS = {block: (c, i) for c, blocks in enumerate(CHUNKS) for i, block in enumerate(blocks)}
NC = len(CHUNKS)
ROWS = 16
ORDER = ((0, 1, 2), (1, 2, 0), (2, 0, 1))
BF = jnp.bfloat16
F32 = jnp.float32


def matmul(left, right, dims=((1,), (0,))):
    return lax.dot_general(left, right, (dims, ((), ())), preferred_element_type=F32)


def far(block):
    return min(block[0], NZ - block[0])


def way_of(block):
    r, xh = block
    return 1 if r < 4 or (r == 4 and xh == 0) else -1


def chained(block):
    return (far(block), block[1]) in CHAIN and block not in DIRECT


def feeder(block):
    r, xh = block
    before = ((r + way_of(block)) % NZ, xh)
    if r == 0 or r == 4 or not chained(before) or way_of(before) != way_of(block):
        return None
    return before


BLOCKS = [(r, xh) for r in range(1, NZ) for xh in range(2)]
HOME = [block for block in BLOCKS if far(block) == 1 or not chained(block)]
HOPS = {1, NZ - 1} | {r for r, xh in BLOCKS if not chained((r, xh)) and (r, xh) not in DIRECT}
HOPS = sorted(HOPS | {NZ - r for r in HOPS})
SIDE = sorted({r for r, _ in DIRECT} | {NZ - r for r, _ in DIRECT})


def kernel(
    tok_in, gro_in, gc_in, gs, uc_in, us, dc_in, ds,
    gt_out, gg_out, gu_out, gd_out, bn_out,
    X, codes_g, codes_u, codes_d, wg, wu, wd, part, rb0, rb1, rb2, rb3, ag, term, zin, xsend, xrecv,
    acc_g, acc_u, acc_d,
    loc_sem, own_sem, xs_sem, ring_s, ring_r, side_s, side_r, wid_s, wid_r, z_s, z_r, xf_sem,
):
    hid, wid = lax.axis_index("hid"), lax.axis_index("wid")
    z, xhi = hid // 2, hid % 2
    y, xlo, core = wid // 4, (wid // 2) % 2, wid % 2
    bit_a, bit_b = (y + y // 2) % 2, y // 2
    bits = (xlo, bit_a, bit_b)
    core_peer = wid + 1 - 2 * core

    def flipped(dims):
        row = (y, y + 1 - 2 * (y % 2), 3 - y, (y + 2) % 4)[(1 in dims) + 2 * (2 in dims)]
        return (row * 2 + (1 - xlo if 0 in dims else xlo)) * 2 + core

    pair_peer = tuple(flipped((d,)) for d in range(3))
    xhi_peer = z * 2 + 1 - xhi

    def z_peer(r):
        return ((z + r) % NZ) * 2 + xhi

    def side_peer(r):
        return ((z + r) % NZ) * 2 + 1 - xhi

    barrier = pltpu.get_barrier_semaphore()
    near = (core_peer,) + pair_peer
    if SPREAD:
        near += tuple(flipped(order[1:]) for order in ORDER)
    across = [xhi_peer] + [z_peer(r) for r in HOPS] + [side_peer(r) for r in SIDE]
    for peer in near:
        pl.semaphore_signal(barrier, inc=1, device_id={"wid": peer}, device_id_type=pl.DeviceIdType.MESH)
    for peer in across:
        pl.semaphore_signal(barrier, inc=1, device_id={"hid": peer}, device_id_type=pl.DeviceIdType.MESH)

    def rows(block, g):
        c, i = POS[block]
        return X.at[c, g, i]

    own = [
        pltpu.make_async_copy(tok_in, rows((0, 0), 0), own_sem.at[0]),
        pltpu.make_async_copy(gro_in, rows((0, 0), 1), own_sem.at[1]),
    ]
    loads = [
        pltpu.make_async_copy(gc_in, codes_g, loc_sem.at[0]),
        pltpu.make_async_copy(uc_in, codes_u, loc_sem.at[1]),
        pltpu.make_async_copy(dc_in, codes_d, loc_sem.at[2]),
    ]
    for copy in own + loads:
        copy.start()
    for copy in own:
        copy.wait()
    pl.semaphore_wait(barrier, len(near) + len(across))

    sends = []

    def remote(src, dst, send, recv, where):
        return pltpu.make_async_remote_copy(
            src_ref=src, dst_ref=dst, send_sem=send, recv_sem=recv,
            device_id=where, device_id_type=pl.DeviceIdType.MESH,
        )

    def go(copy):
        copy.start()
        sends.append(copy)

    x_copy = [
        remote(rows((0, 0), g), rows((0, 1), g), xs_sem.at[0, g], xs_sem.at[1, g], {"hid": xhi_peer}) for g in range(2)
    ]
    ring = {}
    for way, sign in ((0, -1), (1, 1)):
        for j in range(1, 5):
            for xh in range(2):
                for g in range(2):
                    if (j < 4 or g == way) and not (xh == 1 and j in ACROSS):
                        ring[way, j, xh, g] = remote(
                            rows(((sign * (j - 1)) % NZ, xh), g), rows(((sign * j) % NZ, xh), g),
                            ring_s.at[way, j - 1, xh, g], ring_r.at[way, j - 1, xh, g], {"hid": z_peer(-sign)},
                        )

    side = {}
    for way, sign in ((0, -1), (1, 1)):
        for j in ACROSS:
            for g in range(2):
                if j < 4 or g == way:
                    side[way, j, g] = remote(
                        rows(((sign * j) % NZ, 0), g), rows(((sign * j) % NZ, 1), g),
                        side_s.at[way, j - 1, g], side_r.at[way, j - 1, g], {"hid": xhi_peer},
                    )

    def forward(j, xh, g):
        for way in range(2):
            came = side.get((way, j, g)) if xh == 1 and j in ACROSS else ring.get((way, j, xh, g))
            if came is not None:
                came.wait_recv()
        for way in range(2):
            if (way, j + 1, xh, g) in ring:
                go(ring[way, j + 1, xh, g])
        for way in range(2):
            if xh == 0 and (way, j, g) in side:
                go(side[way, j, g])

    def forward_x(g):
        x_copy[g].wait_recv()
        for way in range(2):
            if (way, 1, 1, g) in ring:
                go(ring[way, 1, 1, g])

    def dequant(load, codes, scales, weight):
        load.wait()
        height, cols = weight.shape
        for i in range(height // BLK):
            for j in range(cols // BLK):
                at = (slice(i * BLK, (i + 1) * BLK), slice(j * BLK, (j + 1) * BLK))
                weight[at] = (codes[at].astype(F32) * scales(i, j)).astype(BF)

    for g in range(2):
        go(x_copy[g])
    for g in range(2):
        for way in range(2):
            go(ring[way, 1, 0, g])

    def at_bits(free, other=None):
        index = []
        for d in range(3):
            if d in free:
                index.append(slice(None))
            elif d == other:
                index.append(1 - bits[d])
            else:
                index.append(bits[d])
        return tuple(index)

    def core_sum(c, k):
        return remote(part.at[c, k, 1 - core], rb0.at[c, k], wid_s.at[c, k, 0], wid_r.at[c, k, 0], {"wid": core_peer})

    def pair_sum(c, k, s):
        order = ORDER[k]
        index = at_bits(order[s:], order[s - 1])
        return remote(
            part.at[(c, k, core) + index], (rb1, rb2, rb3)[s - 1].at[c, k],
            wid_s.at[c, k, s], wid_r.at[c, k, s], {"wid": pair_peer[order[s - 1]]},
        )

    def pair_gather(c, k, s):
        order = ORDER[k]
        ref = ag.at[(c, k, core) + at_bits(order[s:])]
        return remote(ref, ref, wid_s.at[c, k, 7 - s], wid_r.at[c, k, 7 - s], {"wid": pair_peer[order[s - 1]]})

    def core_gather(c, k):
        ref = ag.at[c, k, core]
        return remote(ref, ref, wid_s.at[c, k, 7], wid_r.at[c, k, 7], {"wid": core_peer})

    def spread(k, i):
        return ((ORDER[k][1],), (ORDER[k][2],), ORDER[k][1:])[i]

    def spread_sum(c, k, i):
        crossed = spread(k, i)
        index = tuple(1 - bits[d] if d in crossed else bits[d] for d in range(3))
        sem = (2, 3, 8)[i]
        return remote(
            part.at[(c, k, core) + index], spread_slot(c, k, i),
            wid_s.at[c, k, sem], wid_r.at[c, k, sem], {"wid": flipped(crossed)},
        )

    def spread_slot(c, k, i):
        return rb3.at[c, k] if i == 2 else rb2.at[c, k, i]

    def spread_gather(c, k, i):
        ref = ag.at[(c, k, core) + bits]
        sem = (4, 5, 9)[i]
        return remote(ref, ref, wid_s.at[c, k, sem], wid_r.at[c, k, sem], {"wid": flipped(spread(k, i))})

    def add_into(ref, other):
        ref[...] = (ref[...].astype(F32) + other[...].astype(F32)).astype(BF)

    def step_partial(c, k):
        left = X[c, k // 2].reshape(256, 512)
        whole = matmul(left, wd[...], ((1,), (1,))) if k == 2 else matmul(left, (wg, wu)[k][...])
        part[c, k] = whole.astype(BF).reshape(2, 2, 2, 2, ROWS, 896)
        go(core_sum(c, k))

    def step_core(c, k):
        core_sum(c, k).wait_recv()
        add_into(part.at[c, k, core], rb0.at[c, k])
        go(pair_sum(c, k, 1))

    def step_pair(c, k, s):
        pair_sum(c, k, s).wait_recv()
        add_into(part.at[(c, k, core) + at_bits(ORDER[k][s:])], (rb1, rb2)[s - 1].at[c, k])
        if c in SPREAD:
            for i in range(3):
                go(spread_sum(c, k, i))
        else:
            go(pair_sum(c, k, s + 1))

    def step_nonlinear(c):
        sums = []
        for k in range(3):
            total = part[(c, k, core) + bits].astype(F32)
            if c in SPREAD:
                for i in range(3):
                    spread_sum(c, k, i).wait_recv()
                    total += spread_slot(c, k, i)[...].astype(F32)
            else:
                pair_sum(c, k, 3).wait_recv()
                total += rb3[c, k].astype(F32)
            sums.append(total)

        def pass_on(k):
            if c in SPREAD:
                for i in range(3):
                    go(spread_gather(c, k, i))
            else:
                go(pair_gather(c, k, 3))

        gate, upper, grad = sums
        sigma = jax.nn.sigmoid(gate)
        active = gate * sigma
        ag[(c, 1, core) + bits] = (grad * upper * sigma * (1.0 + gate * (1.0 - sigma))).astype(BF)
        pass_on(1)
        ag[(c, 2, core) + bits] = (grad * active).astype(BF)
        pass_on(2)
        ag[(c, 0, core) + bits] = (active * upper).astype(BF)
        pass_on(0)

    def step_gather(c, k, s):
        if c in SPREAD and s == 2:
            for i in range(3):
                spread_gather(c, k, i).wait_recv()
        else:
            pair_gather(c, k, s).wait_recv()
        go(pair_gather(c, k, s - 1) if s > 1 else core_gather(c, k))

    def z_send(block):
        r, xh = block
        c, i = POS[block]
        if block in DIRECT:
            peer = side_peer(r)
        else:
            peer = z_peer(way_of(block) % NZ if chained(block) else r)
        return remote(term.at[c, i], zin.at[r, xh], z_s.at[r, xh], z_r.at[r, xh], {"hid": peer})

    landed = set()

    def landing(c, k):
        if (c, k) not in landed:
            landed.add((c, k))
            core_gather(c, k).wait_recv()
        return ag[c, k].reshape(256, 896)

    def step_term(c):
        total = matmul(landing(c, 1), wg[...], ((1,), (1,)))
        total += matmul(landing(c, 2), wu[...], ((1,), (1,)))
        term[c] = total.astype(BF).reshape(4, 64, 512)

    def step_home(c, r, xh):
        c, i = POS[r, xh]
        before = feeder((r, xh))
        if before is not None:
            z_send(before).wait_recv()
            add_into(term.at[c, i], zin.at[before])
        go(z_send((r, xh)))

    def home_sum(xh):
        total = term[POS[0, xh]].astype(F32)
        for block in HOME:
            if (0 if block in DIRECT else block[1]) == xh:
                z_send(block).wait_recv()
                total += zin[block].astype(F32)
        return total

    last = remote(xsend, xrecv, xf_sem.at[0], xf_sem.at[1], {"hid": xhi_peer})

    def step_cross():
        xsend[...] = home_sum(1).astype(BF)
        go(last)

    def step_last():
        total = home_sum(0)
        last.wait_recv()
        gt_out[...] = (total + xrecv[...].astype(F32)).astype(BF)

    def block_sums(full):
        height, cols = full.shape
        sums = jnp.sum((full * full).reshape(height // BLK, BLK, cols), axis=1)
        of_block = (
            lax.broadcasted_iota(jnp.int32, (cols // BLK, cols), 1) // BLK
            == lax.broadcasted_iota(jnp.int32, (cols // BLK, cols), 0)
        ).astype(F32)
        return sums, of_block

    def exact(left, right):
        return lax.dot_general(
            left, right, (((1,), (1,)), ((), ())), precision=lax.Precision.HIGHEST, preferred_element_type=F32
        )

    seen = {0: 0, 1: 0, 2: 0}

    def step_grad(c, k):
        d = landing(c, k)
        if k == 0:
            full = matmul(d, X[c, 1].reshape(256, 512), ((0,), (0,)))
        else:
            full = matmul(X[c, 0].reshape(256, 512), d, ((0,), (0,)))
        acc = (acc_d, acc_g, acc_u)[k]
        if seen[k]:
            full += acc[...]
        seen[k] += 1
        if seen[k] < NC:
            acc[...] = full
            return
        out, row = ((gd_out, 2), (gg_out, 0), (gu_out, 1))[k]
        out[...] = full.astype(BF)
        sums, of_block = block_sums(full)
        bn_out[row] = exact(of_block, sums) if k == 0 else exact(sums, of_block)

    do = {
        "Dq": lambda k: dequant(
            loads[k],
            (codes_g, codes_u, codes_d)[k],
            (lambda i, j: gs[i, j], lambda i, j: us[i, j], lambda i, j: ds[j, i])[k],
            (wg, wu, wd)[k],
        ),
        "Fx": forward_x,
        "F": forward,
        "S": step_partial,
        "C": step_core,
        "P1": lambda c, k: step_pair(c, k, 1),
        "P2": lambda c, k: step_pair(c, k, 2),
        "N": step_nonlinear,
        "A3": lambda c, k: step_gather(c, k, 3),
        "A2": lambda c, k: step_gather(c, k, 2),
        "A1": lambda c, k: step_gather(c, k, 1),
        "T": step_term,
        "Z": step_home,
        "G": step_grad,
        "X": step_cross,
        "E": step_last,
    }
    for name, *at in STEPS:
        if name == "E":
            for copy in sends:
                copy.wait_send()
        do[name](*at)


def body(tokens, grad_out, gate_codes, gate_scale, up_codes, up_scale, down_codes, down_scale):
    hbm = pl.BlockSpec(memory_space=pl.ANY)
    smem = pl.BlockSpec(memory_space=pltpu.SMEM)
    vmem = pl.BlockSpec(memory_space=pltpu.VMEM)
    dma = pltpu.SemaphoreType.DMA
    blocks = (ROWS, 896)
    shapes = (
        jax.ShapeDtypeStruct((64, 512), BF),
        jax.ShapeDtypeStruct((512, 896), BF),
        jax.ShapeDtypeStruct((512, 896), BF),
        jax.ShapeDtypeStruct((896, 512), BF),
        jax.ShapeDtypeStruct((3, 4, 7), F32),
    )
    found = pl.pallas_call(
        kernel,
        out_shape=tuple(pltpu.VMEM(shape.shape, shape.dtype) for shape in shapes),
        in_specs=[hbm, hbm, hbm, smem, hbm, smem, hbm, smem],
        out_specs=(vmem,) * 5,
        scratch_shapes=[
            pltpu.VMEM((NC, 2, 4, 64, 512), BF),
            pltpu.VMEM((512, 896), BF),
            pltpu.VMEM((512, 896), BF),
            pltpu.VMEM((896, 512), BF),
            pltpu.VMEM((512, 896), BF),
            pltpu.VMEM((512, 896), BF),
            pltpu.VMEM((896, 512), BF),
            pltpu.VMEM((NC, 3, 2, 2, 2, 2) + blocks, BF),
            pltpu.VMEM((NC, 3, 2, 2, 2) + blocks, BF),
            pltpu.VMEM((NC, 3, 2, 2) + blocks, BF),
            pltpu.VMEM((NC, 3, 2) + blocks, BF),
            pltpu.VMEM((NC, 3) + blocks, BF),
            pltpu.VMEM((NC, 3, 2, 2, 2, 2) + blocks, BF),
            pltpu.VMEM((NC, 4, 64, 512), BF),
            pltpu.VMEM((NZ, 2, 64, 512), BF),
            pltpu.VMEM((64, 512), BF),
            pltpu.VMEM((64, 512), BF),
            pltpu.VMEM((512, 896), F32),
            pltpu.VMEM((512, 896), F32),
            pltpu.VMEM((896, 512), F32),
            dma((3,)),
            dma((2,)),
            dma((2, 2)),
            dma((2, 4, 2, 2)),
            dma((2, 4, 2, 2)),
            dma((2, 4, 2)),
            dma((2, 4, 2)),
            dma((NC, 3, 10)),
            dma((NC, 3, 10)),
            dma((NZ, 2)),
            dma((NZ, 2)),
            dma((2,)),
        ],
        compiler_params=pltpu.CompilerParams(
            collective_id=0, has_side_effects=True, vmem_limit_bytes=60 * 1024 * 1024
        ),
    )(tokens, grad_out, gate_codes, gate_scale, up_codes, up_scale, down_codes, down_scale.T)
    return found


def solution(mesh):
    in_specs = (
        P("hid", "wid"),
        P("hid", "wid"),
        P("wid", "hid"),
        P("wid", "hid"),
        P("wid", "hid"),
        P("wid", "hid"),
        P("hid", "wid"),
        P("hid", "wid"),
    )
    out_specs = (
        P("hid", "wid"),
        P("wid", "hid"),
        P("wid", "hid"),
        P("hid", "wid"),
        P(None, "wid", "hid"),
    )
    return jax.shard_map(body, mesh=mesh, in_specs=in_specs, out_specs=out_specs, check_vma=False)
```
